32 devices in a mesh: dom: 2 (over x), dp: 2 (over core), seq: 8 (over z, y).
Axes of the slice: x: 2, y: 2, z: 4, core: 2. Of those that a mesh axis runs over, the one named last changes fastest.
Arguments:
- queries: bfloat16 [4096, 64, 128], P(('dom', 'dp', 'seq')), parts along dimension 0, may hold values from -1024 to 1024
- out_grad: bfloat16 [4096, 64, 128], P(('dom', 'dp', 'seq')), parts along dimension 0, may hold values from -24 to 24
- cache_keys: float32 [4096, 8, 128], P(('dom', 'dp', 'seq')), parts along dimension 0, may hold values from -12 to 12
- cache_values: float32 [4096, 8, 128], P(('dom', 'dp', 'seq')), parts along dimension 0, may hold values from -6 to 6
- exponents: int32 [4096, 2, 8], P(('dom', 'dp', 'seq')), parts along dimension 0, may hold values from 4 to 6
- outliers: int32 [16, 128], P('dom'), parts along dimension 0, may hold values from 0 to 2047, as said below
Outputs:
- query_grad: bfloat16 [4096, 64, 128], P(('dom', 'dp', 'seq')), parts along dimension 0
- key_grad: float32 [4096, 8, 128], P(('dom', 'dp', 'seq')), parts along dimension 0
- value_grad: float32 [4096, 8, 128], P(('dom', 'dp', 'seq')), parts along dimension 0
The draws below stay inside these ranges and needn't reach their ends.
There are 2 independent parts, one for each index of `dom`. The reference program is written for one: setup_inputs(seed, part) draws one part's arguments, and reference() takes and returns one part's arrays. A program takes and returns all parts, laid end to end along the dimension named above; each array names one. Nothing has to cross between parts.
Inputs may be any that keep to these rules, and one draw needn't show every extreme that they name: `outliers`: each row holds 128 different slot numbers.
All inputs are finite; a program needn't handle non-finite values.
Results may differ from the reference program's by a relative error of at most 0.0062.
Values may be sent and summed in bfloat16 or wider, within the bound.
A program may use at most 128 MiB of HBM per device.

```python
import math
import jax
import jax.numpy as jnp
from jax import lax

HEADS = 64
KV_HEADS = 8
HEAD_DIM = 128
SLOTS = 2048
OUTLIERS = 128
TOKENS = 2048


def key_parts(key):
    base = jax.random.fold_in(key, 101)
    normal = jax.random.normal(jax.random.fold_in(base, 1), (SLOTS, KV_HEADS, HEAD_DIM), jnp.float32)
    normal = jnp.clip(normal, -4.0, 4.0)
    scales = jnp.exp(jax.random.uniform(jax.random.fold_in(base, 2), (SLOTS, KV_HEADS, 1), jnp.float32, math.log(0.3), math.log(3.0)))
    return (normal, scales)


def draw_cache_keys(key, part):
    normal, scales = key_parts(key)
    return normal * scales


def draw_queries(key, part):
    base = jax.random.fold_in(key, 202)
    row_scale = jnp.exp(jax.random.uniform(jax.random.fold_in(base, 1), (TOKENS, HEADS, 1), jnp.float32, math.log(0.3), math.log(3.0)))
    normal = jax.random.normal(jax.random.fold_in(base, 5), (TOKENS, HEADS, HEAD_DIM), jnp.float32)
    return (jnp.clip(normal, -4.0, 4.0) * row_scale).astype(jnp.bfloat16)


def draw_outliers(key, part):
    head_keys = jax.random.split(jax.random.fold_in(key, 303), KV_HEADS)
    picked = jax.vmap(lambda one_key: jax.random.permutation(one_key, SLOTS)[:OUTLIERS])(head_keys)
    return picked.astype(jnp.int32)


def with_ends(values, rng, low, largest):
    longest = values.shape.index(max(values.shape))
    spots = []
    for shift in (0, 1):
        where = [jax.random.randint(jax.random.fold_in(rng, axis), (), 0, length) for axis, length in enumerate(values.shape)]
        where[longest] = (where[longest] + shift) % values.shape[longest]
        spots.append(tuple(where))
    return values.at[spots[0]].set(low).at[spots[1]].set(largest)


def block_scale(key, dims, cuts, low, top_value):
    loudness = 1.0
    for position, blocks in cuts:
        steps = jax.random.uniform(jax.random.fold_in(jax.random.fold_in(key, 6), position), (blocks,), jnp.float32, low / len(cuts), top_value / len(cuts))
        loudness = loudness * jnp.repeat(jnp.exp(steps), dims[position] // blocks).reshape((-1,) + (1,) * (len(dims) - 1 - position))
    return loudness


def noise(stream_key, extent, scale, most, shards=(), kind=jnp.bfloat16):
    entries = scale * jax.random.normal(stream_key, extent, jnp.float32)
    if shards:
        entries = entries * block_scale(stream_key, extent, shards, -0.22, 0.18)
    return jnp.clip(entries, -most, most).astype(kind)


def setup_inputs(seed: int = 0, part: int = 0) -> dict:
    streams_of = jax.random.split(jax.random.key(seed), 7)
    own_keys = jax.random.split(jax.random.fold_in(streams_of[6], part), 7)
    return {
        "queries": draw_queries(jax.random.fold_in(jax.random.fold_in(streams_of[6], part), 71), part),
        "out_grad": noise(own_keys[1], (TOKENS, HEADS, HEAD_DIM), 4.0, 24.0, ((0, 16),)),
        "cache_keys": draw_cache_keys(jax.random.fold_in(jax.random.fold_in(streams_of[6], part), 71), part),
        "cache_values": noise(own_keys[3], (SLOTS, KV_HEADS, HEAD_DIM), 1.0, 6.0, ((0, 16),), jnp.float32),
        "exponents": with_ends(jax.random.randint(own_keys[4], (SLOTS, 2, KV_HEADS), 4, 7), jax.random.fold_in(own_keys[4], 1), 4, 6).astype(jnp.int32),
        "outliers": draw_outliers(jax.random.fold_in(jax.random.fold_in(streams_of[6], part), 71), part),
    }


def step_tables(exponent):
    inverse = jnp.zeros(exponent.shape, jnp.float32)
    stepping = jnp.zeros(exponent.shape, jnp.float32)
    for power in range(16):
        hit = exponent == power
        inverse = jnp.where(hit, jnp.float32(2.0 ** power), inverse)
        stepping = jnp.where(hit, jnp.float32(2.0 ** (-power)), stepping)
    return (inverse, stepping)

def fake_quant(cache_part, exponent, marked):
    inverse, stepping = step_tables(exponent)
    levels = jnp.floor(cache_part * inverse[:, :, None] + 0.5)
    kept = jnp.clip(levels, -128.0, 127.0) * stepping[:, :, None]
    used = jnp.where(marked[:, :, None], cache_part, kept).astype(jnp.bfloat16)
    inside = (levels >= -128.0) & (levels <= 127.0)
    passed = jnp.where(marked[:, :, None] | inside, 1.0, 0.0).astype(jnp.float32)
    return (used, passed)

def outlier_mask(outliers, first_slot, count):
    slot_ids = first_slot + jnp.arange(count, dtype=jnp.int32)
    hits = outliers.T[None, :, :] == slot_ids[:, None, None]
    return jnp.any(hits, axis=1)

def attend(query_rows, grad_rows, keys_used, values_used):
    total_rows, width = query_rows.shape
    row_block = math.gcd(total_rows, 512)
    inv_root = 1.0 / math.sqrt(width)
    query_blocks = query_rows.reshape(total_rows // row_block, row_block, width)
    grad_blocks = grad_rows.reshape(total_rows // row_block, row_block, width)
    zero_acc = jnp.zeros(keys_used.shape, jnp.float32)

    def one_block(carry, pieces):
        key_acc, value_acc = carry
        query_piece, grad_piece = pieces
        scores = lax.dot_general(query_piece, keys_used, (((1,), (1,)), ((), ())), preferred_element_type=jnp.float32) * inv_root
        peaks = lax.optimization_barrier(jnp.max(scores, axis=1, keepdims=True))
        weights_raw = jnp.exp(scores - peaks)
        probs = weights_raw / lax.optimization_barrier(jnp.sum(weights_raw, axis=1, keepdims=True))
        probs_low = probs.astype(jnp.bfloat16)
        value_acc = value_acc + lax.dot_general(probs_low, grad_piece, (((0,), (0,)), ((), ())), preferred_element_type=jnp.float32)
        prob_grad = lax.dot_general(grad_piece, values_used, (((1,), (1,)), ((), ())), preferred_element_type=jnp.float32)
        row_delta = lax.optimization_barrier(jnp.sum(probs * prob_grad, axis=1, keepdims=True))
        score_grad = (probs * (prob_grad - row_delta) * inv_root).astype(jnp.bfloat16)
        piece_grad = jnp.dot(score_grad, keys_used, preferred_element_type=jnp.float32).astype(jnp.bfloat16)
        key_acc = key_acc + lax.dot_general(score_grad, query_piece, (((0,), (0,)), ((), ())), preferred_element_type=jnp.float32)
        return ((key_acc, value_acc), piece_grad)
    (key_acc, value_acc), query_grads = lax.scan(one_block, (zero_acc, zero_acc), (query_blocks, grad_blocks))
    return (query_grads.reshape(total_rows, width), key_acc, value_acc)

def reference(queries, out_grad, cache_keys, cache_values, exponents, outliers):
    marked = outlier_mask(outliers, 0, SLOTS)
    key_used, key_pass = fake_quant(cache_keys, exponents[:, 0, :], marked)
    value_used, value_pass = fake_quant(cache_values, exponents[:, 1, :], marked)
    group = HEADS // KV_HEADS
    query_split = queries.reshape(TOKENS, KV_HEADS, group, HEAD_DIM)
    grad_split = out_grad.reshape(TOKENS, KV_HEADS, group, HEAD_DIM)
    query_pieces = []
    key_pieces = []
    value_pieces = []
    for head_kv in range(KV_HEADS):
        rows_grad, key_acc, value_acc = attend(query_split[:, head_kv].reshape(-1, HEAD_DIM), grad_split[:, head_kv].reshape(-1, HEAD_DIM), key_used[:, head_kv], value_used[:, head_kv])
        query_pieces.append(rows_grad.reshape(TOKENS, group, HEAD_DIM))
        key_pieces.append(key_acc)
        value_pieces.append(value_acc)
    query_grad = jnp.stack(query_pieces, axis=1).reshape(TOKENS, HEADS, HEAD_DIM)
    key_grad = jnp.stack(key_pieces, axis=1) * key_pass
    value_grad = jnp.stack(value_pieces, axis=1) * value_pass
    return (query_grad, key_grad, value_grad)
```

```python
import functools
import math

import jax
import jax.numpy as jnp
from jax import lax
from jax.experimental import pallas as pl
from jax.experimental.pallas import tpu as pltpu
from jax.sharding import PartitionSpec as P

TOKEN_BLOCK = 32
HEADS_PER_CALL = 2


def step_tables(exponent):
    inverse = jnp.zeros(exponent.shape, jnp.float32)
    stepping = jnp.zeros(exponent.shape, jnp.float32)
    for power in range(16):
        hit = exponent == power
        inverse = jnp.where(hit, jnp.float32(2.0**power), inverse)
        stepping = jnp.where(hit, jnp.float32(2.0 ** (-power)), stepping)
    return (inverse, stepping)


def fake_quant(cache_part, exponent, marked):
    inverse, stepping = step_tables(exponent)
    levels = jnp.floor(cache_part * inverse[:, :, None] + 0.5)
    kept = jnp.clip(levels, -128.0, 127.0) * stepping[:, :, None]
    used = jnp.where(marked[:, :, None], cache_part, kept).astype(jnp.bfloat16)
    inside = (levels >= -128.0) & (levels <= 127.0)
    passed = jnp.where(marked[:, :, None] | inside, 1.0, 0.0).astype(jnp.float32)
    return (used, passed)


def outlier_mask(outliers, first_slot, count):
    slot_ids = first_slot + jnp.arange(count, dtype=jnp.int32)
    hits = outliers.T[None, :, :] == slot_ids[:, None, None]
    return jnp.any(hits, axis=1)


def dot(a, b, ca, cb):
    return lax.dot_general(a, b, (((ca,), (cb,)), ((), ())), preferred_element_type=jnp.float32)


def attend_kernel(heads, group, q_ref, g_ref, kv_ref, dq_ref, dkv_ref):
    tb, _, width = q_ref.shape
    devices, _, _, part, _ = kv_ref.shape
    slots = devices * part
    rows = tb * group
    inv_root = 1.0 / math.sqrt(width)
    to_exp2 = inv_root * math.log2(math.e)
    q_all = q_ref[...].astype(jnp.float32)
    g_all = g_ref[...].astype(jnp.float32)
    first = pl.program_id(0) == 0
    outs = []
    for h in range(heads):
        q = q_all[:, h * group : (h + 1) * group].reshape(rows, width).astype(jnp.bfloat16)
        g = g_all[:, h * group : (h + 1) * group].reshape(rows, width).astype(jnp.bfloat16)
        k = kv_ref[:, h, 0].reshape(slots, width)
        v = kv_ref[:, h, 1].reshape(slots, width)
        s = dot(k, q, 1, 1)
        peak = jnp.max(s, axis=0, keepdims=True)
        e = jnp.exp2((s - peak) * to_exp2)
        total = jnp.sum(e, axis=0, keepdims=True)
        dp = dot(v, g, 1, 1)
        inv = 1.0 / total
        delta = jnp.sum(e * dp, axis=0, keepdims=True) * inv
        p = e * inv
        dv = dot(p.astype(jnp.bfloat16), g, 1, 0).reshape(devices, part, width)
        ds = (p * (dp - delta)).astype(jnp.bfloat16)
        dk = (dot(ds, q, 1, 0) * inv_root).reshape(devices, part, width)
        dq = dot(k, ds, 0, 0) * inv_root
        outs.append(dq.T.reshape(tb, group, width))

        @pl.when(first)
        def _():
            dkv_ref[:, h, 0] = dk
            dkv_ref[:, h, 1] = dv

        @pl.when(jnp.logical_not(first))
        def _():
            dkv_ref[:, h, 0] += dk
            dkv_ref[:, h, 1] += dv

    dq_ref[...] = jnp.concatenate(outs, axis=1).astype(dq_ref.dtype)


def attend_call(index, heads, group, queries, out_grad, kv_all):
    tokens, _, width = queries.shape
    devices, _, _, part, _ = kv_all.shape
    tb = math.gcd(tokens, TOKEN_BLOCK)
    wide = heads * group
    flops = 10 * tokens * wide * devices * part * width
    return pl.pallas_call(
        functools.partial(attend_kernel, heads, group),
        grid=(tokens // tb,),
        in_specs=[
            pl.BlockSpec((tb, wide, width), lambda i: (i, index, 0)),
            pl.BlockSpec((tb, wide, width), lambda i: (i, index, 0)),
            pl.BlockSpec(kv_all.shape, lambda i: (0, 0, 0, 0, 0)),
        ],
        out_specs=[
            pl.BlockSpec((tb, wide, width), lambda i: (i, 0, 0)),
            pl.BlockSpec(kv_all.shape, lambda i: (0, 0, 0, 0, 0)),
        ],
        out_shape=[
            jax.ShapeDtypeStruct((tokens, wide, width), jnp.bfloat16),
            jax.ShapeDtypeStruct(kv_all.shape, jnp.float32),
        ],
        compiler_params=pltpu.CompilerParams(vmem_limit_bytes=56 << 20),
        cost_estimate=pl.CostEstimate(
            flops=2 * flops, bytes_accessed=12 << 20, transcendentals=tokens * wide * devices * part
        ),
    )(queries, out_grad, kv_all)


def local(queries, out_grad, cache_keys, cache_values, exponents, outliers):
    local_slots, kv_heads, width = cache_keys.shape
    heads = queries.shape[1]
    group = heads // kv_heads
    axes = ("dp", "seq")
    first_slot = lax.axis_index(axes) * local_slots
    marked = outlier_mask(outliers, first_slot, local_slots)
    key_used, key_pass = fake_quant(cache_keys, exponents[:, 0, :], marked)
    value_used, value_pass = fake_quant(cache_values, exponents[:, 1, :], marked)
    kv = jnp.stack([key_used, value_used], axis=0).transpose(2, 0, 1, 3)
    n = HEADS_PER_CALL
    query_grads, shares = [], []
    for c in range(kv_heads // n):
        kv_all = lax.all_gather(kv[c * n : (c + 1) * n], axes, axis=0, tiled=False)
        dq, dkv = attend_call(c, n, group, queries, out_grad, kv_all)
        query_grads.append(dq)
        shares.append(lax.psum_scatter(dkv, axes, scatter_dimension=0, tiled=False))
    query_grad = jnp.concatenate(query_grads, axis=1)
    share = jnp.concatenate(shares, axis=0).transpose(1, 2, 0, 3)
    return (query_grad, share[0] * key_pass, share[1] * value_pass)


def solution(mesh):
    split = P(("dom", "dp", "seq"), None, None)
    return jax.shard_map(
        local,
        mesh=mesh,
        in_specs=(split, split, split, split, split, P("dom", None)),
        out_specs=(split, split, split),
        check_vma=False,
    )
```

```python
import functools
import math

import jax
import jax.numpy as jnp
from jax import lax
from jax.experimental import pallas as pl
from jax.experimental.pallas import tpu as pltpu
from jax.sharding import PartitionSpec as P

TOKEN_BLOCK = 32
HEADS_PER_CALL = 2


def step_tables(exponent):
    inverse = jnp.zeros(exponent.shape, jnp.float32)
    stepping = jnp.zeros(exponent.shape, jnp.float32)
    for power in range(16):
        hit = exponent == power
        inverse = jnp.where(hit, jnp.float32(2.0**power), inverse)
        stepping = jnp.where(hit, jnp.float32(2.0 ** (-power)), stepping)
    return (inverse, stepping)


def fake_quant(cache_part, exponent, marked):
    inverse, stepping = step_tables(exponent)
    levels = jnp.floor(cache_part * inverse[:, :, None] + 0.5)
    kept = jnp.clip(levels, -128.0, 127.0) * stepping[:, :, None]
    used = jnp.where(marked[:, :, None], cache_part, kept).astype(jnp.bfloat16)
    inside = (levels >= -128.0) & (levels <= 127.0)
    passed = jnp.where(marked[:, :, None] | inside, 1.0, 0.0).astype(jnp.float32)
    return (used, passed)


def outlier_mask(outliers, first_slot, count):
    slot_ids = first_slot + jnp.arange(count, dtype=jnp.int32)
    hits = outliers.T[None, :, :] == slot_ids[:, None, None]
    return jnp.any(hits, axis=1)


def dot(a, b, ca, cb):
    return lax.dot_general(a, b, (((ca,), (cb,)), ((), ())), preferred_element_type=jnp.float32)


def attend_kernel(heads, group, q_ref, g_ref, own_ref, other_ref, dq_ref, down_ref, dother_ref):
    tb, _, width = q_ref.shape
    devices, _, _, part, _ = own_ref.shape
    half = devices * part
    rows = tb * group
    inv_root = 1.0 / math.sqrt(width)
    to_exp2 = inv_root * math.log2(math.e)
    q_all = q_ref[...].astype(jnp.float32)
    g_all = g_ref[...].astype(jnp.float32)
    first = pl.program_id(0) == 0
    outs = []
    for h in range(heads):
        q = q_all[:, h * group : (h + 1) * group].reshape(rows, width).astype(jnp.bfloat16)
        g = g_all[:, h * group : (h + 1) * group].reshape(rows, width).astype(jnp.bfloat16)
        k = jnp.concatenate(
            [own_ref[:, h, 0].reshape(half, width), other_ref[:, h, 0].reshape(half, width)], axis=0
        )
        v = jnp.concatenate(
            [own_ref[:, h, 1].reshape(half, width), other_ref[:, h, 1].reshape(half, width)], axis=0
        )
        s = dot(k, q, 1, 1)
        peak = jnp.max(s, axis=0, keepdims=True)
        e = jnp.exp2((s - peak) * to_exp2)
        total = jnp.sum(e, axis=0, keepdims=True)
        dp = dot(v, g, 1, 1)
        inv = 1.0 / total
        delta = jnp.sum(e * dp, axis=0, keepdims=True) * inv
        p = e * inv
        dv = dot(p.astype(jnp.bfloat16), g, 1, 0).reshape(2, devices, part, width)
        ds = (p * (dp - delta)).astype(jnp.bfloat16)
        dk = (dot(ds, q, 1, 0) * inv_root).reshape(2, devices, part, width)
        dq = dot(k, ds, 0, 0) * inv_root
        outs.append(dq.T.reshape(tb, group, width))

        @pl.when(first)
        def _():
            for side, ref in enumerate((down_ref, dother_ref)):
                ref[:, h, 0] = dk[side]
                ref[:, h, 1] = dv[side]

        @pl.when(jnp.logical_not(first))
        def _():
            for side, ref in enumerate((down_ref, dother_ref)):
                ref[:, h, 0] += dk[side]
                ref[:, h, 1] += dv[side]

    dq_ref[...] = jnp.concatenate(outs, axis=1).astype(dq_ref.dtype)


def attend_call(index, heads, group, queries, out_grad, own, other):
    tokens, _, width = queries.shape
    devices, _, _, part, _ = own.shape
    tb = math.gcd(tokens, TOKEN_BLOCK)
    wide = heads * group
    flops = 20 * tokens * wide * devices * part * width
    return pl.pallas_call(
        functools.partial(attend_kernel, heads, group),
        grid=(tokens // tb,),
        in_specs=[
            pl.BlockSpec((tb, wide, width), lambda i: (i, index, 0)),
            pl.BlockSpec((tb, wide, width), lambda i: (i, index, 0)),
            pl.BlockSpec(own.shape, lambda i: (0, 0, 0, 0, 0)),
            pl.BlockSpec(own.shape, lambda i: (0, 0, 0, 0, 0)),
        ],
        out_specs=[
            pl.BlockSpec((tb, wide, width), lambda i: (i, 0, 0)),
            pl.BlockSpec(own.shape, lambda i: (0, 0, 0, 0, 0)),
            pl.BlockSpec(own.shape, lambda i: (0, 0, 0, 0, 0)),
        ],
        out_shape=[
            jax.ShapeDtypeStruct((tokens, wide, width), jnp.bfloat16),
            jax.ShapeDtypeStruct(own.shape, jnp.float32),
            jax.ShapeDtypeStruct(own.shape, jnp.float32),
        ],
        compiler_params=pltpu.CompilerParams(vmem_limit_bytes=56 << 20),
        cost_estimate=pl.CostEstimate(
            flops=2 * flops, bytes_accessed=12 << 20, transcendentals=2 * tokens * wide * devices * part
        ),
    )(queries, out_grad, own, other)


def local(queries, out_grad, cache_keys, cache_values, exponents, outliers):
    local_slots, kv_heads, width = cache_keys.shape
    heads = queries.shape[1]
    group = heads // kv_heads
    axes = ("dp", "seq")
    first_slot = lax.axis_index(axes) * local_slots
    marked = outlier_mask(outliers, first_slot, local_slots)
    key_used, key_pass = fake_quant(cache_keys, exponents[:, 0, :], marked)
    value_used, value_pass = fake_quant(cache_values, exponents[:, 1, :], marked)
    kv = jnp.stack([key_used, value_used], axis=0).transpose(2, 0, 1, 3)
    n = HEADS_PER_CALL
    query_grads, shares = [], []
    swap = [(0, 1), (1, 0)]
    block = (n, 2, local_slots, width)
    for c in range(kv_heads // n):
        flat = kv[c * n : (c + 1) * n].reshape(n * 2 * local_slots, width)
        own = lax.all_gather(flat, "seq", axis=0, tiled=False)
        other = lax.ppermute(own, "dp", swap)
        ranks = own.shape[0]
        dq, down, dother = attend_call(
            c, n, group, queries, out_grad, own.reshape((ranks,) + block), other.reshape((ranks,) + block)
        )
        query_grads.append(dq)
        flat_grad = (ranks, n * 2 * local_slots, width)
        arrived = lax.ppermute(dother.reshape(flat_grad), "dp", swap)
        pair = (down.reshape(flat_grad) + arrived).astype(jnp.bfloat16)
        share = lax.psum_scatter(pair, "seq", scatter_dimension=0, tiled=False)
        shares.append(share.astype(jnp.float32).reshape(block))
    query_grad = jnp.concatenate(query_grads, axis=1)
    share = jnp.concatenate(shares, axis=0).transpose(1, 2, 0, 3)
    return (query_grad, share[0] * key_pass, share[1] * value_pass)


def solution(mesh):
    split = P(("dom", "dp", "seq"), None, None)
    return jax.shard_map(
        local,
        mesh=mesh,
        in_specs=(split, split, split, split, split, P("dom", None)),
        out_specs=(split, split, split),
        check_vma=False,
    )
```

```python
import functools
import math

import jax
import jax.numpy as jnp
from jax import lax
from jax.experimental import pallas as pl
from jax.experimental.pallas import tpu as pltpu
from jax.sharding import PartitionSpec as P

TOKEN_BLOCK = 32
HEADS_PER_CALL = 4
HEADS_PER_STEP = 2


def step_tables(exponent):
    inverse = jnp.zeros(exponent.shape, jnp.float32)
    stepping = jnp.zeros(exponent.shape, jnp.float32)
    for power in range(16):
        hit = exponent == power
        inverse = jnp.where(hit, jnp.float32(2.0**power), inverse)
        stepping = jnp.where(hit, jnp.float32(2.0 ** (-power)), stepping)
    return (inverse, stepping)


def fake_quant(cache_part, exponent, marked):
    inverse, stepping = step_tables(exponent)
    levels = jnp.floor(cache_part * inverse[:, :, None] + 0.5)
    kept = jnp.clip(levels, -128.0, 127.0) * stepping[:, :, None]
    used = jnp.where(marked[:, :, None], cache_part, kept).astype(jnp.bfloat16)
    inside = (levels >= -128.0) & (levels <= 127.0)
    passed = jnp.where(marked[:, :, None] | inside, 1.0, 0.0).astype(jnp.float32)
    return (used, passed)


def outlier_mask(outliers, first_slot, count):
    slot_ids = first_slot + jnp.arange(count, dtype=jnp.int32)
    hits = outliers.T[None, :, :] == slot_ids[:, None, None]
    return jnp.any(hits, axis=1)


def dot(a, b, ca, cb):
    return lax.dot_general(a, b, (((ca,), (cb,)), ((), ())), preferred_element_type=jnp.float32)


def attend_kernel(heads, group, q_ref, g_ref, own_ref, other_ref, dq_ref, down_ref, dother_ref):
    tb, _, width = q_ref.shape
    devices, _, _, part, _ = own_ref.shape
    half = devices * part
    rows = tb * group
    inv_root = 1.0 / math.sqrt(width)
    to_exp2 = inv_root * math.log2(math.e)
    q_all = q_ref[...].astype(jnp.float32)
    g_all = g_ref[...].astype(jnp.float32)
    first = pl.program_id(1) == 0
    outs = []
    for h in range(heads):
        q = q_all[:, h * group : (h + 1) * group].reshape(rows, width).astype(jnp.bfloat16)
        g = g_all[:, h * group : (h + 1) * group].reshape(rows, width).astype(jnp.bfloat16)
        k = jnp.concatenate(
            [own_ref[:, h, 0].reshape(half, width), other_ref[:, h, 0].reshape(half, width)], axis=0
        )
        v = jnp.concatenate(
            [own_ref[:, h, 1].reshape(half, width), other_ref[:, h, 1].reshape(half, width)], axis=0
        )
        s = dot(k, q, 1, 1)
        peak = jnp.max(s, axis=0, keepdims=True)
        e = jnp.exp2((s - peak) * to_exp2)
        total = jnp.sum(e, axis=0, keepdims=True)
        dp = dot(v, g, 1, 1)
        inv = 1.0 / total
        delta = jnp.sum(e * dp, axis=0, keepdims=True) * inv
        p = e * inv
        dv = dot(p.astype(jnp.bfloat16), g, 1, 0).reshape(2, devices, part, width)
        ds = (p * (dp - delta)).astype(jnp.bfloat16)
        dk = (dot(ds, q, 1, 0) * inv_root).reshape(2, devices, part, width)
        dq = dot(k, ds, 0, 0) * inv_root
        outs.append(dq.T.reshape(tb, group, width))

        @pl.when(first)
        def _():
            for side, ref in enumerate((down_ref, dother_ref)):
                ref[:, h, 0] = dk[side]
                ref[:, h, 1] = dv[side]

        @pl.when(jnp.logical_not(first))
        def _():
            for side, ref in enumerate((down_ref, dother_ref)):
                ref[:, h, 0] += dk[side]
                ref[:, h, 1] += dv[side]

    dq_ref[...] = jnp.concatenate(outs, axis=1).astype(dq_ref.dtype)


def attend_call(index, heads, group, queries, out_grad, own, other):
    tokens, _, width = queries.shape
    devices, _, _, part, _ = own.shape
    tb = math.gcd(tokens, TOKEN_BLOCK)
    wide = heads * group
    step = math.gcd(heads, HEADS_PER_STEP)
    pairs = heads // step
    rows = (tb, step * group, width)
    block = (devices, step, 2, part, width)
    flops = 20 * tokens * wide * devices * part * width
    return pl.pallas_call(
        functools.partial(attend_kernel, step, group),
        grid=(pairs, tokens // tb),
        in_specs=[
            pl.BlockSpec(rows, lambda j, i: (i, index * pairs + j, 0)),
            pl.BlockSpec(rows, lambda j, i: (i, index * pairs + j, 0)),
            pl.BlockSpec(block, lambda j, i: (0, j, 0, 0, 0)),
            pl.BlockSpec(block, lambda j, i: (0, j, 0, 0, 0)),
        ],
        out_specs=[
            pl.BlockSpec(rows, lambda j, i: (i, j, 0)),
            pl.BlockSpec(block, lambda j, i: (0, j, 0, 0, 0)),
            pl.BlockSpec(block, lambda j, i: (0, j, 0, 0, 0)),
        ],
        out_shape=[
            jax.ShapeDtypeStruct((tokens, wide, width), jnp.bfloat16),
            jax.ShapeDtypeStruct(own.shape, jnp.float32),
            jax.ShapeDtypeStruct(own.shape, jnp.float32),
        ],
        compiler_params=pltpu.CompilerParams(vmem_limit_bytes=56 << 20),
        cost_estimate=pl.CostEstimate(
            flops=2 * flops, bytes_accessed=12 << 20, transcendentals=2 * tokens * wide * devices * part
        ),
    )(queries, out_grad, own, other)


def local(queries, out_grad, cache_keys, cache_values, exponents, outliers):
    local_slots, kv_heads, width = cache_keys.shape
    heads = queries.shape[1]
    group = heads // kv_heads
    axes = ("dp", "seq")
    first_slot = lax.axis_index(axes) * local_slots
    marked = outlier_mask(outliers, first_slot, local_slots)
    key_used, key_pass = fake_quant(cache_keys, exponents[:, 0, :], marked)
    value_used, value_pass = fake_quant(cache_values, exponents[:, 1, :], marked)
    kv = jnp.stack([key_used, value_used], axis=0).transpose(2, 0, 1, 3)
    n = HEADS_PER_CALL
    query_grads, shares = [], []
    swap = [(0, 1), (1, 0)]
    block = (n, 2, local_slots, width)
    for c in range(kv_heads // n):
        flat = kv[c * n : (c + 1) * n].reshape(n * 2 * local_slots, width)
        own = lax.all_gather(flat, "seq", axis=0, tiled=False)
        other = lax.ppermute(own, "dp", swap)
        ranks = own.shape[0]
        dq, down, dother = attend_call(
            c, n, group, queries, out_grad, own.reshape((ranks,) + block), other.reshape((ranks,) + block)
        )
        query_grads.append(dq)
        flat_grad = (ranks, n * 2 * local_slots, width)
        arrived = lax.ppermute(dother.reshape(flat_grad), "dp", swap)
        pair = (down.reshape(flat_grad) + arrived).astype(jnp.bfloat16)
        share = lax.psum_scatter(pair, "seq", scatter_dimension=0, tiled=False)
        shares.append(share.astype(jnp.float32).reshape(block))
    query_grad = jnp.concatenate(query_grads, axis=1)
    share = jnp.concatenate(shares, axis=0).transpose(1, 2, 0, 3)
    return (query_grad, share[0] * key_pass, share[1] * value_pass)


def solution(mesh):
    split = P(("dom", "dp", "seq"), None, None)
    return jax.shard_map(
        local,
        mesh=mesh,
        in_specs=(split, split, split, split, split, P("dom", None)),
        out_specs=(split, split, split),
        check_vma=False,
    )
```

```python
import functools
import math

import jax
import jax.numpy as jnp
from jax import lax
from jax.experimental import pallas as pl
from jax.experimental.pallas import tpu as pltpu
from jax.sharding import PartitionSpec as P

TOKEN_BLOCK = 32
HEADS_PER_CALL = 4
HEADS_PER_STEP = 2


def step_tables(exponent):
    inverse = jnp.zeros(exponent.shape, jnp.float32)
    stepping = jnp.zeros(exponent.shape, jnp.float32)
    for power in range(16):
        hit = exponent == power
        inverse = jnp.where(hit, jnp.float32(2.0**power), inverse)
        stepping = jnp.where(hit, jnp.float32(2.0 ** (-power)), stepping)
    return (inverse, stepping)


def fake_quant(cache_part, exponent, marked):
    inverse, stepping = step_tables(exponent)
    levels = jnp.floor(cache_part * inverse[:, :, None] + 0.5)
    kept = jnp.clip(levels, -128.0, 127.0) * stepping[:, :, None]
    used = jnp.where(marked[:, :, None], cache_part, kept).astype(jnp.bfloat16)
    inside = (levels >= -128.0) & (levels <= 127.0)
    passed = jnp.where(marked[:, :, None] | inside, 1.0, 0.0).astype(jnp.float32)
    return (used, passed)


def outlier_mask(outliers, first_slot, count):
    slot_ids = first_slot + jnp.arange(count, dtype=jnp.int32)
    hits = outliers.T[None, :, :] == slot_ids[:, None, None]
    return jnp.any(hits, axis=1)


def dot(a, b, ca, cb):
    return lax.dot_general(a, b, (((ca,), (cb,)), ((), ())), preferred_element_type=jnp.float32)


def attend_kernel(heads, group, q_ref, g_ref, own_ref, other_ref, dq_ref, down_ref, dother_ref):
    tb, _, width = q_ref.shape
    devices, _, _, part, _ = own_ref.shape
    half = devices * part
    rows = tb * group
    inv_root = 1.0 / math.sqrt(width)
    to_exp2 = inv_root * math.log2(math.e)
    q_all = q_ref[...].astype(jnp.float32)
    g_all = g_ref[...].astype(jnp.float32)
    first = pl.program_id(1) == 0
    outs = []
    for h in range(heads):
        q = q_all[:, h * group : (h + 1) * group].reshape(rows, width).astype(jnp.bfloat16)
        g = g_all[:, h * group : (h + 1) * group].reshape(rows, width).astype(jnp.bfloat16)
        k = jnp.concatenate(
            [own_ref[:, h, 0].reshape(half, width), other_ref[:, h, 0].reshape(half, width)], axis=0
        )
        v = jnp.concatenate(
            [own_ref[:, h, 1].reshape(half, width), other_ref[:, h, 1].reshape(half, width)], axis=0
        )
        s = dot(k, q, 1, 1)
        peak = jnp.max(s, axis=0, keepdims=True)
        e = jnp.exp2((s - peak) * to_exp2)
        total = jnp.sum(e, axis=0, keepdims=True)
        dp = dot(v, g, 1, 1)
        inv = 1.0 / total
        delta = jnp.sum(e * dp, axis=0, keepdims=True) * inv
        p = e * inv
        dv = dot(p.astype(jnp.bfloat16), g, 1, 0).reshape(2, devices, part, width)
        ds = (p * (dp - delta)).astype(jnp.bfloat16)
        dk = (dot(ds, q, 1, 0) * inv_root).reshape(2, devices, part, width)
        dq = dot(k, ds, 0, 0) * inv_root
        outs.append(dq.T.reshape(tb, group, width))

        @pl.when(first)
        def _():
            for side, ref in enumerate((down_ref, dother_ref)):
                ref[:, h, 0] = dk[side]
                ref[:, h, 1] = dv[side]

        @pl.when(jnp.logical_not(first))
        def _():
            for side, ref in enumerate((down_ref, dother_ref)):
                ref[:, h, 0] += dk[side]
                ref[:, h, 1] += dv[side]

    dq_ref[...] = jnp.concatenate(outs, axis=1).astype(dq_ref.dtype)


def attend_call(index, heads, group, queries, out_grad, own, other):
    tokens, _, width = queries.shape
    devices, _, _, part, _ = own.shape
    tb = math.gcd(tokens, TOKEN_BLOCK)
    wide = heads * group
    step = math.gcd(heads, HEADS_PER_STEP)
    pairs = heads // step
    rows = (tb, step * group, width)
    block = (devices, step, 2, part, width)
    flops = 20 * tokens * wide * devices * part * width
    return pl.pallas_call(
        functools.partial(attend_kernel, step, group),
        grid=(pairs, tokens // tb),
        in_specs=[
            pl.BlockSpec(rows, lambda j, i: (i, index * pairs + j, 0)),
            pl.BlockSpec(rows, lambda j, i: (i, index * pairs + j, 0)),
            pl.BlockSpec(block, lambda j, i: (0, j, 0, 0, 0)),
            pl.BlockSpec(block, lambda j, i: (0, j, 0, 0, 0)),
        ],
        out_specs=[
            pl.BlockSpec(rows, lambda j, i: (i, j, 0)),
            pl.BlockSpec(block, lambda j, i: (0, j, 0, 0, 0)),
            pl.BlockSpec(block, lambda j, i: (0, j, 0, 0, 0)),
        ],
        out_shape=[
            jax.ShapeDtypeStruct((tokens, wide, width), jnp.bfloat16),
            jax.ShapeDtypeStruct(own.shape, jnp.float32),
            jax.ShapeDtypeStruct(own.shape, jnp.float32),
        ],
        compiler_params=pltpu.CompilerParams(vmem_limit_bytes=56 << 20),
        cost_estimate=pl.CostEstimate(
            flops=2 * flops, bytes_accessed=12 << 20, transcendentals=2 * tokens * wide * devices * part
        ),
    )(queries, out_grad, own, other)


def local(queries, out_grad, cache_keys, cache_values, exponents, outliers):
    local_slots, kv_heads, width = cache_keys.shape
    heads = queries.shape[1]
    group = heads // kv_heads
    axes = ("dp", "seq")
    first_slot = lax.axis_index(axes) * local_slots
    marked = outlier_mask(outliers, first_slot, local_slots)
    key_used, key_pass = fake_quant(cache_keys, exponents[:, 0, :], marked)
    value_used, value_pass = fake_quant(cache_values, exponents[:, 1, :], marked)
    kv = jnp.stack([key_used, value_used], axis=0).transpose(2, 0, 1, 3)
    n = HEADS_PER_CALL
    query_grads, pairs = [], []
    swap = [(0, 1), (1, 0)]
    block = (n, 2, local_slots, width)
    for c in range(kv_heads // n):
        flat = kv[c * n : (c + 1) * n].reshape(n * 2 * local_slots, width)
        own = lax.all_gather(flat, "seq", axis=0, tiled=False)
        other = lax.ppermute(own, "dp", swap)
        ranks = own.shape[0]
        dq, down, dother = attend_call(
            c, n, group, queries, out_grad, own.reshape((ranks,) + block), other.reshape((ranks,) + block)
        )
        query_grads.append(dq)
        flat_grad = (ranks, n * 2 * local_slots, width)
        arrived = lax.ppermute(dother.reshape(flat_grad), "dp", swap)
        pair = (down.reshape(flat_grad) + arrived).astype(jnp.bfloat16)
        pairs.append(pair)
    both = jnp.concatenate(pairs, axis=1)
    share = lax.psum_scatter(both, "seq", scatter_dimension=0, tiled=False)
    share = share.astype(jnp.float32).reshape(kv_heads, 2, local_slots, width).transpose(1, 2, 0, 3)
    query_grad = jnp.concatenate(query_grads, axis=1)
    return (query_grad, share[0] * key_pass, share[1] * value_pass)


def solution(mesh):
    split = P(("dom", "dp", "seq"), None, None)
    return jax.shard_map(
        local,
        mesh=mesh,
        in_specs=(split, split, split, split, split, P("dom", None)),
        out_specs=(split, split, split),
        check_vma=False,
    )
```
